1024 devices in a mesh: dp: 16 (over x, z_hi, core), expert: 64 (over y, z_lo).
Axes of the slice: x: 4, y: 8, z: 16 (z_hi: 2, z_lo: 8; z = z_hi * 8 + z_lo), core: 2. Of those that a mesh axis runs over, the one named last changes fastest.
Arguments:
- tokens: bfloat16 [16384, 4096], P('expert'), may hold values from -6 to 6
- expert_ids: int32 [16384, 8], P('expert'), may hold values from 0 to 255, as said below
- combine_weight: float32 [16384, 8], P('expert'), may hold values from 0.1 to 1
- old_plan: int32 [64], replicated, may hold values from 0 to 255, as said below
- new_plan: int32 [64], replicated, may hold values from 0 to 255, as said below
- gate_weight: bfloat16 [64, 4096, 2048], P('expert', None, 'dp'), may hold values from -0.09375 to 0.09375
- up_weight: bfloat16 [64, 4096, 2048], P('expert', None, 'dp'), may hold values from -0.09375 to 0.09375
- down_weight: bfloat16 [64, 2048, 4096], P('expert', 'dp'), may hold values from -0.125 to 0.125
- shared_gate: bfloat16 [4096, 2048], P(None, 'dp'), may hold values from -0.09375 to 0.09375
- shared_up: bfloat16 [4096, 2048], P(None, 'dp'), may hold values from -0.09375 to 0.09375
- shared_down: bfloat16 [2048, 4096], P('dp'), may hold values from -0.125 to 0.125
Outputs:
- mixed_out: bfloat16 [16384, 4096], P('expert', 'dp')
The draws below stay inside these ranges and needn't reach their ends.
Inputs may be any that keep to these rules, and one draw needn't show every extreme that they name: `old_plan`: the 64 experts are different. `new_plan`: slot s holds old_plan[s] or old_plan[s - 1] (slot 0 may take from slot 63); slots 0, 32 and 63 change; apart from slots 0 and 63, two neighbouring slots never both change. `expert_ids`: the 8 experts of a token are different; the tokens of one device send at most 2 kept routes to the slots of one expert together, and some slot gets exactly 2 from the tokens of every device.
All inputs are finite; a program needn't handle non-finite values.
Results may differ from the reference program's by a relative error of at most 0.014.
Values may be sent and summed in bfloat16 or wider, within the bound.
A program may use at most 64 MiB of HBM per device.

```python
import jax
import jax.numpy as jnp
from jax import lax

D = 4096
H = 2048
EXPERTS = 256
TOPK = 8
CAP = 2
TOK_DEV = 256
SLOTS = 64
TOKENS = 16384
N_DP = 16


def plans_of(key):
    shuffled = jax.random.permutation(jax.random.fold_in(key, 101), EXPERTS)
    older = shuffled[:SLOTS].astype(jnp.int32)
    places = jnp.arange(SLOTS)
    middle = SLOTS // 2
    inner = (places >= 2) & (places <= SLOTS - 3)
    inner = inner & (places != middle - 1) & (places != middle) & (places != middle + 1)
    marks = (jax.random.randint(jax.random.fold_in(key, 102), (SLOTS,), 0, 4) == 0) & inner
    changed = marks & jnp.logical_not(jnp.roll(marks, 1))
    changed = changed | (places == 0) | (places == SLOTS - 1) | (places == middle)
    newer = jnp.where(changed, jnp.roll(older, 1), older).astype(jnp.int32)
    return (older, newer)


def routing_of(key):
    older, newer = plans_of(key)
    slot_row = jnp.arange(SLOTS)
    same_slot = newer[:, None] == newer[None, :]
    slot_rank = jnp.sum((same_slot & (slot_row[None, :] < slot_row[:, None])).astype(jnp.int32), axis=1)
    slot_copies = jnp.sum(same_slot.astype(jnp.int32), axis=1)
    counts = jax.random.randint(jax.random.fold_in(key, 201), (SLOTS, SLOTS), 0, CAP + 1)
    counts = jnp.where((slot_rank > 0)[None, :], 0, counts)
    fill_scores = jax.random.randint(jax.random.fold_in(key, 202), (SLOTS,), 0, 1 << 20)
    filled = jnp.argmax(jnp.where(slot_copies == 1, fill_scores, -1))
    counts = jnp.where(slot_row[None, :] == filled, CAP, counts)
    ends = jnp.cumsum(counts, axis=1)
    entries = jnp.arange(TOK_DEV)
    listed = jnp.sum((ends[:, None, :] <= entries[None, :, None]).astype(jnp.int32), axis=2)
    device_keys = jax.random.split(jax.random.fold_in(key, 203), SLOTS)
    shuffles = jax.vmap(lambda one_key: jax.random.permutation(one_key, TOK_DEV))(device_keys)
    slot_token = jnp.take_along_axis(listed, shuffles, axis=1)
    resident = slot_token < SLOTS
    safe_slot = jnp.minimum(slot_token, SLOTS - 1)
    expert_here = newer[safe_slot]
    in_plan = jnp.sum((newer[:, None] == jnp.arange(EXPERTS)[None, :]).astype(jnp.int32), axis=0) > 0
    scores = jax.random.randint(jax.random.fold_in(key, 204), (SLOTS, TOK_DEV, EXPERTS), 0, 1 << 20) * EXPERTS + jnp.arange(EXPERTS)[None, None, :]
    scores = jnp.where(in_plan[None, None, :], -1, scores)
    others = lax.top_k(scores, TOPK)[1].astype(jnp.int32)
    spot = jax.random.randint(jax.random.fold_in(key, 205), (SLOTS, TOK_DEV), 0, TOPK)
    at_spot = (jnp.arange(TOPK)[None, None, :] == spot[:, :, None]) & resident[:, :, None]
    chosen_ids = jnp.where(at_spot, expert_here[:, :, None], others).astype(jnp.int32)
    return chosen_ids.reshape(TOKENS, TOPK)


def draw_old_plan(key, part):
    return plans_of(key)[0]


def draw_new_plan(key, part):
    return plans_of(key)[1]


def draw_expert_ids(key, part):
    return routing_of(key)


def block_levels(own_key, shape, shards, smallest, high):
    def one(axis_at, blocks):
        draws = jax.random.uniform(jax.random.fold_in(jax.random.fold_in(own_key, 6), axis_at), (blocks,), jnp.float32, smallest / len(shards), high / len(shards))
        return jnp.repeat(jnp.exp(draws), shape[axis_at] // blocks).reshape((-1,) + (1,) * (len(shape) - axis_at - 1))

    loudness = one(*shards[0])
    for cut in shards[1:]:
        loudness = loudness * one(*cut)
    return loudness


def centred(rng, dims, scale, reach, shards=(), held_as=jnp.bfloat16):
    result = scale * jax.random.normal(rng, dims, jnp.float32)
    if shards:
        result = result * block_levels(rng, dims, shards, -0.22, 0.18)
    return jnp.clip(result, -reach, reach).astype(held_as)


def setup_inputs(seed: int = 0) -> dict:
    seeds = jax.random.split(jax.random.key(seed), 12)
    tokens = centred(seeds[0], (TOKENS, D), 1.0, 6.0, ((0, 64),))
    expert_ids = draw_expert_ids(jax.random.fold_in(seeds[11], 71), 0)
    combine_weight = jnp.clip(0.1 + 0.9 * jax.random.uniform(seeds[2], (TOKENS, TOPK), jnp.float32) ** block_levels(seeds[2], (TOKENS, TOPK), ((0, 64),), -0.2, 0.2), 0.1, 1.0)
    old_plan = draw_old_plan(jax.random.fold_in(seeds[11], 71), 0)
    new_plan = draw_new_plan(jax.random.fold_in(seeds[11], 71), 0)
    gate_weight = centred(seeds[5], (SLOTS, D, H), D ** -0.5, 0.09375, ((0, 64), (2, 16)))
    up_weight = centred(seeds[6], (SLOTS, D, H), D ** -0.5, 0.09375, ((0, 64), (2, 16)))
    down_weight = centred(seeds[7], (SLOTS, H, D), H ** -0.5, 0.125, ((0, 64), (1, 16)))
    shared_gate = centred(seeds[8], (D, H), D ** -0.5, 0.09375, ((1, 16),))
    shared_up = centred(seeds[9], (D, H), D ** -0.5, 0.09375, ((1, 16),))
    shared_down = centred(seeds[10], (H, D), H ** -0.5, 0.125, ((0, 16),))
    return dict(tokens=tokens, expert_ids=expert_ids, combine_weight=combine_weight, old_plan=old_plan, new_plan=new_plan, gate_weight=gate_weight, up_weight=up_weight, down_weight=down_weight, shared_gate=shared_gate, shared_up=shared_up, shared_down=shared_down)


def route_slots(expert_ids, token_index, new_plan):
    matches = (expert_ids[:, :, None] == new_plan[None, None, :]).astype(jnp.int32)
    counted = jnp.sum(matches, axis=2, keepdims=True)
    before = jnp.cumsum(matches, axis=2) - matches
    wanted = jnp.remainder(token_index[:, None, None], jnp.maximum(counted, 1))
    return matches * (before == wanted).astype(jnp.int32)


def silu_product(row_block, gate_full, up_full):
    gate_value = jnp.dot(row_block, gate_full, preferred_element_type=jnp.float32)
    up_value = jnp.dot(row_block, up_full, preferred_element_type=jnp.float32)
    return (jax.nn.silu(gate_value) * up_value).astype(jnp.bfloat16)


def blocked_expert(row_block, gate_full, up_full, down_full):
    hidden = silu_product(row_block, gate_full, up_full)
    width_block = H // N_DP
    summed = jnp.zeros((row_block.shape[0], down_full.shape[1]), jnp.float32)
    for block_index in range(N_DP):
        offset = block_index * width_block
        partial_value = jnp.dot(hidden[:, offset:offset + width_block], down_full[offset:offset + width_block], preferred_element_type=jnp.float32).astype(jnp.bfloat16)
        partial_value = lax.optimization_barrier(partial_value)
        summed = summed + partial_value.astype(jnp.float32)
    return summed


def reference(tokens, expert_ids, combine_weight, old_plan, new_plan, gate_weight, up_weight, down_weight, shared_gate, shared_up, shared_down):
    token_index = jnp.arange(TOKENS, dtype=jnp.int32)
    chosen = route_slots(expert_ids, token_index, new_plan)
    slot_index = jnp.arange(SLOTS, dtype=jnp.int32)
    present = jnp.sum(chosen, axis=2)
    target = jnp.sum(chosen * slot_index[None, None, :], axis=2)
    flat_slot = jnp.where(present > 0, target, SLOTS).reshape(-1).astype(jnp.int32)
    flat_weight = combine_weight.reshape(-1)
    changed = (new_plan != old_plan).astype(jnp.int32)
    source = jnp.remainder(slot_index - changed, SLOTS).astype(jnp.int32)
    limit = CAP * SLOTS

    def one_slot(slot):
        found = jnp.nonzero(flat_slot == slot, size=limit, fill_value=0)[0].astype(jnp.int32)
        valid = (flat_slot[found] == slot).astype(jnp.float32)
        owner = (found // TOPK).astype(jnp.int32)
        row_block = tokens[owner]
        anchor = source[slot]
        output = blocked_expert(row_block, gate_weight[anchor], up_weight[anchor], down_weight[anchor])
        return owner, output * (flat_weight[found] * valid)[:, None]

    owners, contribution = lax.map(one_slot, slot_index)
    routed = jnp.zeros((TOKENS, D), jnp.float32).at[owners.reshape(-1)].add(contribution.reshape(-1, D))
    shared = blocked_expert(tokens, shared_gate, shared_up, shared_down)
    return (shared + routed).astype(jnp.bfloat16)
```

```python
import jax
import jax.numpy as jnp
from jax import lax
from jax.experimental import pallas as pl
from jax.experimental.pallas import tpu as pltpu
from jax.sharding import PartitionSpec as P

MESH = pl.DeviceIdType.MESH
BF16 = jnp.bfloat16
F32 = jnp.float32

NX, NY, NZ, NL = 4, 8, 16, 8
TOK = 256
D = 4096
HB = 128
SLOTS = 64
ROWS = 128
CH = 512
FB = 256


def dot(a, b):
    return jnp.dot(a, b, preferred_element_type=F32)


def gated(g, u):
    return (g / (1.0 + jnp.exp(-g)) * u).astype(BF16)


def kernel(
    tokens_in, ids_in, cw_in, old_in, new_in, gate_in, up_in, down_in, sgate_in, sup_in, sdown_in,
    out_ref,
    tokens, ids, cw, old, new, wgu, swgu, down, sdown,
    gbuf, abuf, bbuf, xrows, hid, shid,
    s_send, s_recv, s_mid, s_own, z_send, z_mid, z_recv,
    p_own, p_send, p_recv, p_mid, rbuf, dbuf, ysend, ebuf, wcomb,
    lsem, y_ss, y_rs, z_ss, z_rs, a_ss, a_rs, b_ss, b_rs, x_ss, x_rs, r_ss, r_rs, v_ss, v_rs,
    t_ss, t_rs, u_ss, u_rs,
):
    d = lax.axis_index("dp")
    e = lax.axis_index("expert")
    x = lax.div(d, 4)
    zh = lax.rem(lax.div(d, 2), 2)
    c = lax.rem(d, 2)
    y = lax.div(e, NL)
    zl = lax.rem(e, NL)
    z = zh * NL + zl
    xa = x + 1 - 2 * lax.rem(x, 2)
    xb = 3 - x
    xo = lax.rem(x + 2, NX)
    oc = 1 - c

    def dev(x_, y_, z_, c_):
        return (x_ * 4 + lax.div(z_, NL) * 2 + c_, y_ * NL + lax.rem(z_, NL))

    sib = dev(x, y, z, oc)
    dev_a = dev(xa, y, z, c)
    dev_b = dev(xb, y, z, c)

    def load(src, dst, i):
        copy = pltpu.make_async_copy(src, dst, lsem.at[i])
        copy.start()
        return copy

    l_old = load(old_in, old, 0)
    l_new = load(new_in, new, 1)
    l_ids = load(ids_in, ids, 2)
    l_cw = load(cw_in, cw, 3)
    l_tok = load(tokens_in, tokens, 4)
    l_sg = load(sgate_in, swgu.at[:, pl.ds(0, HB)], 5)
    l_su = load(sup_in, swgu.at[:, pl.ds(HB, HB)], 6)
    l_sd = load(sdown_in, sdown.at[c], 7)
    l_g = load(gate_in.at[0], wgu.at[:, pl.ds(0, HB)], 8)
    l_u = load(up_in.at[0], wgu.at[:, pl.ds(HB, HB)], 9)
    l_d = load(down_in.at[0], down.at[c], 10)

    barrier = pltpu.get_barrier_semaphore()
    peers = [sib, dev_a, dev_b]
    peers += [dev(x, lax.rem(y + r, NY), z, c) for r in range(1, NY)]
    peers += [dev(x, y, lax.rem(z + r, NZ), c) for r in range(1, NZ)]
    for peer in peers:
        pl.semaphore_signal(barrier, inc=1, device_id=peer, device_id_type=MESH)

    sends = []

    def send(src, dst, ss, rs, peer):
        copy = pltpu.make_async_remote_copy(
            src_ref=src, dst_ref=dst, send_sem=ss, recv_sem=rs, device_id=peer, device_id_type=MESH
        )
        copy.start()
        sends.append(copy)

    def arrived(dst, ss, rs):
        pltpu.make_async_remote_copy(
            src_ref=dst, dst_ref=dst, send_sem=ss, recv_sem=rs, device_id=sib, device_id_type=MESH
        ).wait_recv()

    l_old.wait()
    l_new.wait()
    lane8 = lax.broadcasted_iota(jnp.int32, (8, ROWS), 1)
    slot8 = lax.div(lane8, 2)

    held = jnp.full((8, ROWS), -1, jnp.int32)
    for s in range(SLOTS):
        held = jnp.where(slot8 == s, old[s], held)
    kept = jnp.zeros((8, ROWS), jnp.bool_)
    for s in range(SLOTS):
        kept = kept | (held == new[s])
    held = jnp.where(kept, held, -1).astype(F32)[0:1, :]
    held = jnp.transpose(jnp.broadcast_to(held, (ROWS, ROWS))).astype(jnp.int32)
    held = jnp.concatenate([held, held], axis=1)
    l_ids.wait()
    l_cw.wait()
    match = jnp.zeros((ROWS, TOK), F32)
    weight = jnp.zeros((ROWS, TOK), F32)
    for k in range(8):
        hit = ids[k : k + 1, :] == held
        match = match + jnp.where(hit, 1.0, 0.0)
        weight = weight + jnp.where(hit, cw[k : k + 1, :], 0.0)
    upper = jnp.where(
        lax.broadcasted_iota(jnp.int32, (TOK, TOK), 0) < lax.broadcasted_iota(jnp.int32, (TOK, TOK), 1),
        1.0, 0.0,
    ).astype(BF16)
    before = dot(match.astype(BF16), upper)
    place = lax.rem(lax.broadcasted_iota(jnp.int32, (ROWS, TOK), 0), 2).astype(F32)
    here = jnp.where(before == place, 1.0, 0.0)
    pick = (match * here).astype(BF16)
    weight = weight * here
    row = lax.broadcasted_iota(jnp.int32, (ROWS, ROWS), 0)
    col = lax.broadcasted_iota(jnp.int32, (ROWS, ROWS), 1)
    swapped = lax.rem(lax.div(row, 2), 8) * 16 + lax.div(row, 16) * 2 + lax.rem(row, 2)
    swap = jnp.where(col == swapped, 1.0, 0.0).astype(BF16)

    l_tok.wait()
    chunk = tokens[:, pl.ds(pl.multiple_of(x * 1024 + c * CH, CH), CH)]
    gbuf[...] = dot(pick, chunk).astype(BF16).reshape(NY, 16, CH)
    abuf[y] = gbuf[y]

    pl.semaphore_wait(barrier, len(peers))
    for r in range(1, NY):
        to = lax.rem(y + r, NY)
        send(gbuf.at[to], abuf.at[y], y_ss.at[r], y_rs.at[r], dev(x, to, z, c))
    send(sdown_in, sdown.at[c], a_ss.at[0], a_rs.at[0], sib)
    send(down_in.at[0], down.at[c], a_ss.at[1], a_rs.at[1], sib)

    weight = jnp.transpose(weight)
    high = weight.astype(BF16)
    wcomb[0] = high
    wcomb[1] = (weight - high.astype(F32)).astype(BF16)

    l_sg.wait()
    l_su.wait()
    both = dot(tokens[...], swgu[...])
    shid[c] = gated(both[:, :HB], both[:, HB:])
    send(shid.at[c], shid.at[c], a_ss.at[2], a_rs.at[2], sib)

    for r in range(1, NY):
        frm = lax.rem(y + NY - r, NY)
        arrived(abuf.at[frm], y_ss.at[r], y_rs.at[r])
    bbuf[...] = dot(swap, abuf[...].reshape(ROWS, CH)).astype(BF16).reshape(NL, 16, CH)
    steps = [1, 15, 2, 14, 3, 13, 4 + 8 * c]
    for i, step in enumerate(steps):
        to = lax.rem(z + step, NZ)
        send(bbuf.at[lax.rem(to, NL)], xrows.at[c, x, zl], z_ss.at[i], z_rs.at[i], dev(x, y, to, c))
    xrows[c, x, zl] = bbuf[zl]

    l_sd.wait()
    arrived(sdown.at[oc], a_ss.at[0], a_rs.at[0])
    arrived(shid.at[oc], a_ss.at[2], a_rs.at[2])
    sh0 = shid[0]
    sh1 = shid[1]

    def columns(ref, core, x_, half):
        at = pl.multiple_of(x_ * 1024 + half * CH + c * FB, FB)
        return ref[core, :, pl.ds(at, FB)]

    def shared_part(x_, half):
        return dot(sh0, columns(sdown, 0, x_, half)) + dot(sh1, columns(sdown, 1, x_, half))

    HR = TOK // 2
    for half in range(2):
        part = shared_part(xo, half).astype(BF16)
        s_send[0, half] = part[:HR]
        s_send[1, half] = part[HR:]
    send(s_send.at[0], s_recv.at[0], b_ss.at[0], b_rs.at[0], dev_a)
    send(s_send.at[1], s_recv.at[1], b_ss.at[1], b_rs.at[1], dev_b)
    for half in range(2):
        part = shared_part(xa, half)
        s_send[2, half] = part[:HR].astype(BF16)
        s_mid[0, half] = part[HR:]
        part = shared_part(xb, half)
        s_send[3, half] = part[HR:].astype(BF16)
        s_mid[1, half] = part[:HR]
    send(s_send.at[2], s_recv.at[2], b_ss.at[2], b_rs.at[2], dev_a)
    send(s_send.at[3], s_recv.at[3], b_ss.at[3], b_rs.at[3], dev_b)
    for half in range(2):
        s_own[half] = shared_part(x, half)

    for i, step in enumerate(steps):
        frm = lax.rem(z + NZ - step, NZ)
        arrived(xrows.at[c, x, lax.rem(frm, NL)], z_ss.at[i], z_rs.at[i])

    def rows_of(x_, half):
        return xrows.at[c, x_, pl.ds(half * 4, 4)]

    send(rows_of(x, 0), rows_of(x, 0), x_ss.at[0], x_rs.at[0], dev_a)
    send(rows_of(x, 1), rows_of(x, 1), x_ss.at[1], x_rs.at[1], dev_b)
    send(rows_of(x, 1), rows_of(x, 1), x_ss.at[2], x_rs.at[2], dev_a)
    send(rows_of(x, 0), rows_of(x, 0), x_ss.at[3], x_rs.at[3], dev_b)
    send(xrows.at[c, x], xrows.at[c, x], a_ss.at[3], a_rs.at[3], sib)

    l_g.wait()
    l_u.wait()

    def product(core, x_):
        at = pl.multiple_of(x_ * 1024 + core * CH, CH)
        return dot(xrows[core, x_].reshape(ROWS, CH), wgu[pl.ds(at, CH), :])

    acc = product(c, x)
    arrived(rows_of(xa, 0), x_ss.at[0], x_rs.at[0])
    send(rows_of(xa, 0), rows_of(xa, 0), x_ss.at[4], x_rs.at[4], dev_b)
    arrived(rows_of(xb, 1), x_ss.at[1], x_rs.at[1])
    send(rows_of(xb, 1), rows_of(xb, 1), x_ss.at[5], x_rs.at[5], dev_a)
    arrived(rows_of(xa, 1), x_ss.at[2], x_rs.at[2])
    send(xrows.at[c, xa], xrows.at[c, xa], a_ss.at[4], a_rs.at[4], sib)
    arrived(rows_of(xb, 0), x_ss.at[3], x_rs.at[3])
    send(xrows.at[c, xb], xrows.at[c, xb], a_ss.at[5], a_rs.at[5], sib)
    acc = acc + product(c, xa) + product(c, xb)

    arrived(s_recv.at[0], b_ss.at[0], b_rs.at[0])
    s_send[5] = (s_mid[1] + s_recv[0].astype(F32)).astype(BF16)
    send(s_send.at[5], s_recv.at[5], b_ss.at[5], b_rs.at[5], dev_b)
    arrived(s_recv.at[1], b_ss.at[1], b_rs.at[1])
    s_send[4] = (s_mid[0] + s_recv[1].astype(F32)).astype(BF16)
    send(s_send.at[4], s_recv.at[4], b_ss.at[4], b_rs.at[4], dev_a)

    arrived(rows_of(xo, 0), x_ss.at[4], x_rs.at[4])
    send(rows_of(xo, 0), rows_of(xo, 0), a_ss.at[6], a_rs.at[6], sib)
    arrived(rows_of(xo, 1), x_ss.at[5], x_rs.at[5])
    send(rows_of(xo, 1), rows_of(xo, 1), a_ss.at[7], a_rs.at[7], sib)
    acc = acc + product(c, xo)
    arrived(xrows.at[oc, x], a_ss.at[3], a_rs.at[3])
    acc = acc + product(oc, x)
    arrived(xrows.at[oc, xa], a_ss.at[4], a_rs.at[4])
    acc = acc + product(oc, xa)
    arrived(xrows.at[oc, xb], a_ss.at[5], a_rs.at[5])
    acc = acc + product(oc, xb)
    arrived(xrows.at[oc, xo, pl.ds(0, 4)], a_ss.at[6], a_rs.at[6])
    arrived(xrows.at[oc, xo, pl.ds(4, 4)], a_ss.at[7], a_rs.at[7])
    acc = acc + product(oc, xo)
    hid[c] = gated(acc[:, :HB], acc[:, HB:])
    send(hid.at[c], hid.at[c], a_ss.at[8], a_rs.at[8], sib)

    for i in range(2, 6):
        arrived(s_recv.at[i], b_ss.at[i], b_rs.at[i])
    first = s_own[:, :HR, :] + s_recv[2].astype(F32) + s_recv[5].astype(F32)
    second = s_own[:, HR:, :] + s_recv[3].astype(F32) + s_recv[4].astype(F32)
    s_own[:, :HR, :] = first
    s_own[:, HR:, :] = second
    z_send[...] = s_own[1 - zh].astype(BF16)
    dev_up = dev(x, y, lax.rem(z + 4, NZ), c)
    dev_dn = dev(x, y, lax.rem(z + 12, NZ), c)
    send(z_send.at[pl.ds(0, HR)], z_mid.at[pl.ds(0, HR)], t_ss.at[0], t_rs.at[0], dev_up)
    send(z_send.at[pl.ds(HR, HR)], z_mid.at[pl.ds(HR, HR)], t_ss.at[1], t_rs.at[1], dev_dn)

    l_d.wait()
    arrived(down.at[oc], a_ss.at[1], a_rs.at[1])
    arrived(hid.at[oc], a_ss.at[8], a_rs.at[8])
    h0 = hid[0]
    h1 = hid[1]

    def route_part(x_, half):
        return dot(h0, columns(down, 0, x_, half)) + dot(h1, columns(down, 1, x_, half))

    HP = ROWS // 2
    for half in range(2):
        part = route_part(xo, half).astype(BF16)
        p_send[0, half] = part[:HP]
        p_send[1, half] = part[HP:]
    send(p_send.at[0], p_recv.at[0], r_ss.at[0], r_rs.at[0], dev_a)
    send(p_send.at[1], p_recv.at[1], r_ss.at[1], r_rs.at[1], dev_b)
    for half in range(2):
        part = route_part(xa, half)
        p_send[2, half] = part[:HP].astype(BF16)
        p_mid[0, half] = part[HP:]
        part = route_part(xb, half)
        p_send[3, half] = part[HP:].astype(BF16)
        p_mid[1, half] = part[:HP]
    send(p_send.at[2], p_recv.at[2], r_ss.at[2], r_rs.at[2], dev_a)
    send(p_send.at[3], p_recv.at[3], r_ss.at[3], r_rs.at[3], dev_b)
    for half in range(2):
        p_own[half] = route_part(x, half)

    arrived(p_recv.at[0], r_ss.at[0], r_rs.at[0])
    p_send[5] = (p_mid[1] + p_recv[0].astype(F32)).astype(BF16)
    send(p_send.at[5], p_recv.at[5], r_ss.at[5], r_rs.at[5], dev_b)
    arrived(p_recv.at[1], r_ss.at[1], r_rs.at[1])
    p_send[4] = (p_mid[0] + p_recv[1].astype(F32)).astype(BF16)
    send(p_send.at[4], p_recv.at[4], r_ss.at[4], r_rs.at[4], dev_a)

    arrived(z_mid.at[pl.ds(0, HR)], t_ss.at[0], t_rs.at[0])
    send(z_mid.at[pl.ds(0, HR)], z_recv.at[pl.ds(0, HR)], t_ss.at[2], t_rs.at[2], dev_up)
    arrived(z_mid.at[pl.ds(HR, HR)], t_ss.at[1], t_rs.at[1])
    send(z_mid.at[pl.ds(HR, HR)], z_recv.at[pl.ds(HR, HR)], t_ss.at[3], t_rs.at[3], dev_dn)

    for i in range(2, 6):
        arrived(p_recv.at[i], r_ss.at[i], r_rs.at[i])
    first = p_own[:, :HP, :] + p_recv[2].astype(F32) + p_recv[5].astype(F32)
    second = p_own[:, HP:, :] + p_recv[3].astype(F32) + p_recv[4].astype(F32)
    rbuf[:, :4] = first.astype(BF16).reshape(2, 4, 16, FB)
    rbuf[:, 4:] = second.astype(BF16).reshape(2, 4, 16, FB)

    order = [8, 7, 9, 6, 10, 5, 11, 4, 12, 3, 13, 2, 14, 1, 15]
    for step in order:
        to = lax.rem(z + step, NZ)
        send(rbuf.at[lax.div(to, NL), lax.rem(to, NL)], dbuf.at[z], v_ss.at[step], v_rs.at[step], dev(x, y, to, c))
    dbuf[z] = rbuf[zh, zl]

    for i in range(2):
        part = pl.ds(i * HR, HR)
        arrived(z_recv.at[part], t_ss.at[2 + i], t_rs.at[2 + i])
    shared = s_own[zh] + z_recv[...].astype(F32)

    for step in order:
        frm = lax.rem(z + NZ - step, NZ)
        arrived(dbuf.at[frm], v_ss.at[step], v_rs.at[step])
    total = (dbuf[0:NL].astype(F32) + dbuf[NL:NZ].astype(F32)).astype(BF16)
    ysend[...] = dot(swap, total.reshape(ROWS, FB)).astype(BF16).reshape(NY, 16, FB)
    for r in range(1, NY):
        to = lax.rem(y + r, NY)
        send(ysend.at[to], ebuf.at[y], u_ss.at[r], u_rs.at[r], dev(x, to, z, c))
    ebuf[y] = ysend[y]
    for r in range(1, NY):
        frm = lax.rem(y + NY - r, NY)
        arrived(ebuf.at[frm], u_ss.at[r], u_rs.at[r])
    back = ebuf[...].reshape(ROWS, FB)
    out_ref[...] = (shared + dot(wcomb[0], back) + dot(wcomb[1], back)).astype(BF16)

    for copy in sends:
        copy.wait_send()


def local(
    tokens, expert_ids, combine_weight, old_plan, new_plan, gate_weight, up_weight, down_weight,
    shared_gate, shared_up, shared_down,
):
    dma = pltpu.SemaphoreType.DMA
    vmem = pltpu.VMEM
    return pl.pallas_call(
        kernel,
        out_shape=jax.ShapeDtypeStruct((TOK, FB), BF16),
        in_specs=[pl.BlockSpec(memory_space=pltpu.HBM)] * 11,
        out_specs=pl.BlockSpec(memory_space=pltpu.VMEM),
        scratch_shapes=[
            vmem((TOK, D), BF16),
            vmem((8, TOK), jnp.int32),
            vmem((8, TOK), F32),
            pltpu.SMEM((SLOTS,), jnp.int32),
            pltpu.SMEM((SLOTS,), jnp.int32),
            vmem((D, 2 * HB), BF16),
            vmem((D, 2 * HB), BF16),
            vmem((2, HB, D), BF16),
            vmem((2, HB, D), BF16),
            vmem((NY, 16, CH), BF16),
            vmem((NY, 16, CH), BF16),
            vmem((NL, 16, CH), BF16),
            vmem((2, NX, NL, 16, CH), BF16),
            vmem((2, ROWS, HB), BF16),
            vmem((2, TOK, HB), BF16),
            vmem((6, 2, TOK // 2, FB), BF16),
            vmem((6, 2, TOK // 2, FB), BF16),
            vmem((2, 2, TOK // 2, FB), F32),
            vmem((2, TOK, FB), F32),
            vmem((TOK, FB), BF16),
            vmem((TOK, FB), BF16),
            vmem((TOK, FB), BF16),
            vmem((2, ROWS, FB), F32),
            vmem((6, 2, ROWS // 2, FB), BF16),
            vmem((6, 2, ROWS // 2, FB), BF16),
            vmem((2, 2, ROWS // 2, FB), F32),
            vmem((2, NL, 16, FB), BF16),
            vmem((NZ, 16, FB), BF16),
            vmem((NY, 16, FB), BF16),
            vmem((NY, 16, FB), BF16),
            vmem((2, TOK, ROWS), BF16),
            dma((11,)),
            dma((8,)), dma((8,)),
            dma((7,)), dma((7,)),
            dma((9,)), dma((9,)),
            dma((6,)), dma((6,)),
            dma((6,)), dma((6,)),
            dma((6,)), dma((6,)),
            dma((16,)), dma((16,)),
            dma((4,)), dma((4,)),
            dma((8,)), dma((8,)),
        ],
        compiler_params=pltpu.CompilerParams(
            collective_id=0, has_side_effects=True, vmem_limit_bytes=60 * 2**20
        ),
        cost_estimate=pl.CostEstimate(flops=2 * 10**9, bytes_accessed=12 * 2**20, transcendentals=10**5),
    )(
        tokens, expert_ids.T, combine_weight.T, old_plan, new_plan, gate_weight, up_weight, down_weight,
        shared_gate, shared_up, shared_down,
    )


def solution(mesh):
    in_specs = (
        P("expert", None),
        P("expert", None),
        P("expert", None),
        P(),
        P(),
        P("expert", None, "dp"),
        P("expert", None, "dp"),
        P("expert", "dp", None),
        P(None, "dp"),
        P(None, "dp"),
        P("dp", None),
    )
    out_specs = P("expert", "dp")
    return jax.shard_map(local, mesh=mesh, in_specs=in_specs, out_specs=out_specs, check_vma=False)
```

```python
import jax
import jax.numpy as jnp
from jax import lax
from jax.experimental import pallas as pl
from jax.experimental.pallas import tpu as pltpu
from jax.sharding import PartitionSpec as P

MESH = pl.DeviceIdType.MESH
BF16 = jnp.bfloat16
F32 = jnp.float32

NX, NY, NZ, NL = 4, 8, 16, 8
TOK = 256
D = 4096
HB = 128
SLOTS = 64
ROWS = 128
CH = 512
FB = 256


def dot(a, b):
    return jnp.dot(a, b, preferred_element_type=F32)


def gated(g, u):
    return (g / (1.0 + jnp.exp(-g)) * u).astype(BF16)


def kernel(
    tokens_in, ids_in, cw_in, old_in, new_in, gate_in, up_in, down_in, sgate_in, sup_in, sdown_in,
    out_ref,
    tokens, chunk, ids, cw, old, new, wgu, swgu, down, sdown,
    gbuf, abuf, bbuf, xrows, hid, shid,
    s_send, s_recv, s_mid, s_own, z_send, z_recv,
    p_own, p_send, p_recv, rbuf, dbuf, ysend, ebuf, wcomb,
    lsem, y_ss, y_rs, z_ss, z_rs, a_ss, a_rs, b_ss, b_rs, x_ss, x_rs, r_ss, r_rs, v_ss, v_rs,
    t_ss, t_rs, u_ss, u_rs,
):
    d = lax.axis_index("dp")
    e = lax.axis_index("expert")
    x = lax.div(d, 4)
    zh = lax.rem(lax.div(d, 2), 2)
    c = lax.rem(d, 2)
    y = lax.div(e, NL)
    zl = lax.rem(e, NL)
    z = zh * NL + zl
    xa = x + 1 - 2 * lax.rem(x, 2)
    xb = 3 - x
    xo = lax.rem(x + 2, NX)
    oc = 1 - c

    def dev(x_, y_, z_, c_):
        return (x_ * 4 + lax.div(z_, NL) * 2 + c_, y_ * NL + lax.rem(z_, NL))

    sib = dev(x, y, z, oc)
    dev_a = dev(xa, y, z, c)
    dev_b = dev(xb, y, z, c)
    dev_o = dev(xo, y, z, c)
    across = (dev_a, dev_b, dev_o)
    places = (xa, xb, xo)

    def load(src, dst, i):
        copy = pltpu.make_async_copy(src, dst, lsem.at[i])
        copy.start()
        return copy

    l_old = load(old_in, old, 0)
    l_new = load(new_in, new, 1)
    l_ids = load(ids_in, ids, 2)
    l_cw = load(cw_in, cw, 3)
    l_chunk = load(tokens_in.at[:, pl.ds(pl.multiple_of(x * 1024 + c * CH, CH), CH)], chunk, 4)
    l_sg = load(sgate_in, swgu.at[:, pl.ds(0, HB)], 5)
    l_su = load(sup_in, swgu.at[:, pl.ds(HB, HB)], 6)
    l_tok = load(tokens_in, tokens, 7)

    barrier = pltpu.get_barrier_semaphore()
    peers = [sib, dev_a, dev_b, dev_o]
    peers += [dev(x, lax.rem(y + r, NY), z, c) for r in range(1, NY)]
    peers += [dev(x, y, lax.rem(z + r, NZ), c) for r in range(1, NZ)]
    for peer in peers:
        pl.semaphore_signal(barrier, inc=1, device_id=peer, device_id_type=MESH)

    sends = []

    def send(src, dst, ss, rs, peer):
        copy = pltpu.make_async_remote_copy(
            src_ref=src, dst_ref=dst, send_sem=ss, recv_sem=rs, device_id=peer, device_id_type=MESH
        )
        copy.start()
        sends.append(copy)

    def arrived(dst, ss, rs):
        pltpu.make_async_remote_copy(
            src_ref=dst, dst_ref=dst, send_sem=ss, recv_sem=rs, device_id=sib, device_id_type=MESH
        ).wait_recv()

    l_old.wait()
    l_new.wait()
    lane8 = lax.broadcasted_iota(jnp.int32, (8, ROWS), 1)
    slot8 = lax.div(lane8, 2)

    held = jnp.full((8, ROWS), -1, jnp.int32)
    for s in range(SLOTS):
        held = jnp.where(slot8 == s, old[s], held)
    kept = jnp.zeros((8, ROWS), jnp.bool_)
    for s in range(SLOTS):
        kept = kept | (held == new[s])
    held = jnp.where(kept, held, -1).astype(F32)[0:1, :]
    held = jnp.transpose(jnp.broadcast_to(held, (ROWS, ROWS))).astype(jnp.int32)
    held = jnp.concatenate([held, held], axis=1)
    l_ids.wait()
    l_cw.wait()
    match = jnp.zeros((ROWS, TOK), F32)
    weight = jnp.zeros((ROWS, TOK), F32)
    for k in range(8):
        hit = ids[k : k + 1, :] == held
        match = match + jnp.where(hit, 1.0, 0.0)
        weight = weight + jnp.where(hit, cw[k : k + 1, :], 0.0)
    upper = jnp.where(
        lax.broadcasted_iota(jnp.int32, (TOK, TOK), 0) < lax.broadcasted_iota(jnp.int32, (TOK, TOK), 1),
        1.0, 0.0,
    ).astype(BF16)
    before = dot(match.astype(BF16), upper)
    place = lax.rem(lax.broadcasted_iota(jnp.int32, (ROWS, TOK), 0), 2).astype(F32)
    here = jnp.where(before == place, 1.0, 0.0)
    pick = (match * here).astype(BF16)
    weight = weight * here
    row = lax.broadcasted_iota(jnp.int32, (ROWS, ROWS), 0)
    col = lax.broadcasted_iota(jnp.int32, (ROWS, ROWS), 1)
    swapped = lax.rem(lax.div(row, 2), 8) * 16 + lax.div(row, 16) * 2 + lax.rem(row, 2)
    swap = jnp.where(col == swapped, 1.0, 0.0).astype(BF16)

    l_chunk.wait()
    for f in range(2):
        gbuf[f] = dot(pick, chunk[:, f * FB : (f + 1) * FB]).astype(BF16).reshape(NY, 16, FB)
        abuf[f, y] = gbuf[f, y]
        if f == 0:
            pl.semaphore_wait(barrier, len(peers))
        for r in range(1, NY):
            to = lax.rem(y + r, NY)
            send(gbuf.at[f, to], abuf.at[f, y], y_ss.at[f, r], y_rs.at[f, r], dev(x, to, z, c))
    l_sd = load(sdown_in, sdown.at[c], 8)
    send(sdown_in, sdown.at[c], a_ss.at[0], a_rs.at[0], sib)
    l_g = load(gate_in.at[0], wgu.at[:, pl.ds(0, HB)], 9)
    l_u = load(up_in.at[0], wgu.at[:, pl.ds(HB, HB)], 10)

    weight = jnp.transpose(weight)
    high = weight.astype(BF16)
    wcomb[0] = high
    wcomb[1] = (weight - high.astype(F32)).astype(BF16)

    l_sg.wait()
    l_su.wait()
    l_tok.wait()
    both = dot(tokens[...], swgu[...])
    shid[c] = gated(both[:, :HB], both[:, HB:])
    send(shid.at[c], shid.at[c], a_ss.at[2], a_rs.at[2], sib)

    steps = [1, 15, 2, 14, 3, 13, 4 + 8 * c]
    for f in range(2):
        for r in range(1, NY):
            frm = lax.rem(y + NY - r, NY)
            arrived(abuf.at[f, frm], y_ss.at[f, r], y_rs.at[f, r])
        bbuf[f] = dot(swap, abuf[f].reshape(ROWS, FB)).astype(BF16).reshape(NL, 16, FB)
        for i, step in enumerate(steps):
            to = lax.rem(z + step, NZ)
            send(bbuf.at[f, lax.rem(to, NL)], xrows.at[c, x, f, zl], z_ss.at[f, i], z_rs.at[f, i], dev(x, y, to, c))
        xrows[c, x, f, zl] = bbuf[f, zl]
    l_d = load(down_in.at[0], down.at[c], 11)
    send(down_in.at[0], down.at[c], a_ss.at[1], a_rs.at[1], sib)

    l_sd.wait()
    arrived(sdown.at[oc], a_ss.at[0], a_rs.at[0])
    arrived(shid.at[oc], a_ss.at[2], a_rs.at[2])
    sh0 = shid[0]
    sh1 = shid[1]

    def columns(ref, core, x_, half):
        at = pl.multiple_of(x_ * 1024 + half * CH + c * FB, FB)
        return ref[core, :, pl.ds(at, FB)]

    def shared_part(x_, half):
        return dot(sh0, columns(sdown, 0, x_, half)) + dot(sh1, columns(sdown, 1, x_, half))

    HR = TOK // 2
    halves = (1 - zh, zh)

    def shared_first(k):
        part = shared_part(xo, halves[k]).astype(BF16)
        s_send[k, 0] = part[:HR]
        s_send[k, 1] = part[HR:]
        part = shared_part(xa, halves[k])
        s_send[k, 2] = part[:HR].astype(BF16)
        s_mid[k, 0] = part[HR:]
        part = shared_part(xb, halves[k])
        s_send[k, 3] = part[HR:].astype(BF16)
        s_mid[k, 1] = part[:HR]
        for i in range(4):
            send(s_send.at[k, i], s_recv.at[k, i], b_ss.at[k, i], b_rs.at[k, i], across[i % 2])
        s_own[k] = shared_part(x, halves[k])

    def shared_second(k):
        arrived(s_recv.at[k, 0], b_ss.at[k, 0], b_rs.at[k, 0])
        s_send[k, 5] = (s_mid[k, 1] + s_recv[k, 0].astype(F32)).astype(BF16)
        send(s_send.at[k, 5], s_recv.at[k, 5], b_ss.at[k, 5], b_rs.at[k, 5], dev_b)
        arrived(s_recv.at[k, 1], b_ss.at[k, 1], b_rs.at[k, 1])
        s_send[k, 4] = (s_mid[k, 0] + s_recv[k, 1].astype(F32)).astype(BF16)
        send(s_send.at[k, 4], s_recv.at[k, 4], b_ss.at[k, 4], b_rs.at[k, 4], dev_a)

    def shared_last(k):
        for i in range(2, 6):
            arrived(s_recv.at[k, i], b_ss.at[k, i], b_rs.at[k, i])
        s_own[k, :HR] = s_own[k, :HR] + s_recv[k, 2].astype(F32) + s_recv[k, 5].astype(F32)
        s_own[k, HR:] = s_own[k, HR:] + s_recv[k, 3].astype(F32) + s_recv[k, 4].astype(F32)

    shared_first(0)

    for f in range(2):
        for i, step in enumerate(steps):
            frm = lax.rem(z + NZ - step, NZ)
            arrived(xrows.at[c, x, f, lax.rem(frm, NL)], z_ss.at[f, i], z_rs.at[f, i])
        piece = xrows.at[c, x, f]
        for i in (2, 0, 1):
            send(piece, piece, x_ss.at[f, i], x_rs.at[f, i], across[i])
        send(piece, piece, a_ss.at[4 + f], a_rs.at[4 + f], sib)
        if f == 0:
            shared_second(0)

    l_g.wait()
    l_u.wait()

    def product(core, x_, f):
        at = pl.multiple_of(x_ * 1024 + core * CH + f * FB, FB)
        return dot(xrows[core, x_, f].reshape(ROWS, FB), wgu[pl.ds(at, FB), :])

    acc = product(c, x, 0) + product(c, x, 1)
    for f in range(2):
        for i in range(3):
            piece = xrows.at[c, places[i], f]
            arrived(piece, x_ss.at[f, i], x_rs.at[f, i])
            send(piece, piece, a_ss.at[6 + 3 * f + i], a_rs.at[6 + 3 * f + i], sib)
            acc = acc + product(c, places[i], f)
        if f == 0:
            shared_last(0)
            z_send[...] = s_own[0].astype(BF16)
            send(z_send, z_recv, t_ss.at[0], t_rs.at[0], dev(x, y, lax.rem(z + NL, NZ), c))
    shared_first(1)

    for f in range(2):
        arrived(xrows.at[oc, x, f], a_ss.at[4 + f], a_rs.at[4 + f])
        acc = acc + product(oc, x, f)
    for f in range(2):
        for i in range(3):
            arrived(xrows.at[oc, places[i], f], a_ss.at[6 + 3 * f + i], a_rs.at[6 + 3 * f + i])
            acc = acc + product(oc, places[i], f)
    hid[c] = gated(acc[:, :HB], acc[:, HB:])
    send(hid.at[c], hid.at[c], a_ss.at[3], a_rs.at[3], sib)

    l_d.wait()
    arrived(down.at[oc], a_ss.at[1], a_rs.at[1])
    arrived(hid.at[oc], a_ss.at[3], a_rs.at[3])
    h0 = hid[0]
    h1 = hid[1]

    def route_part(x_, half):
        return dot(h0, columns(down, 0, x_, half)) + dot(h1, columns(down, 1, x_, half))

    for k in range(2):
        half = halves[k]
        for i in (2, 0, 1):
            p_send[k, i] = route_part(places[i], half).astype(BF16)
            send(p_send.at[k, i], p_recv.at[k, i], r_ss.at[k, i], r_rs.at[k, i], across[i])
        p_own[k] = route_part(x, half)

    shared_second(1)
    for k in range(2):
        half = halves[k]
        total = p_own[k]
        for i in range(3):
            arrived(p_recv.at[k, i], r_ss.at[k, i], r_rs.at[k, i])
            total = total + p_recv[k, i].astype(F32)
        rbuf[k] = total.astype(BF16).reshape(NL, 16, FB)
        for r in range(k, NL):
            to = lax.rem(zl + r, NL)
            at = (1 - k) * NL + r
            send(rbuf.at[k, to], dbuf.at[z], v_ss.at[at], v_rs.at[at], dev(x, y, half * NL + to, c))
    dbuf[z] = rbuf[1, zl]

    shared_last(1)
    arrived(z_recv, t_ss.at[0], t_rs.at[0])
    shared = s_own[1] + z_recv[...].astype(F32)

    for k in range(2):
        half = halves[k]
        for r in range(k, NL):
            frm = half * NL + lax.rem(zl + NL - r, NL)
            at = (1 - k) * NL + r
            arrived(dbuf.at[frm], v_ss.at[at], v_rs.at[at])
    total = (dbuf[0:NL].astype(F32) + dbuf[NL:NZ].astype(F32)).astype(BF16)
    ysend[...] = dot(swap, total.reshape(ROWS, FB)).astype(BF16).reshape(NY, 16, FB)
    for r in range(1, NY):
        to = lax.rem(y + r, NY)
        send(ysend.at[to], ebuf.at[y], u_ss.at[r], u_rs.at[r], dev(x, to, z, c))
    ebuf[y] = ysend[y]
    for r in range(1, NY):
        frm = lax.rem(y + NY - r, NY)
        arrived(ebuf.at[frm], u_ss.at[r], u_rs.at[r])
    back = ebuf[...].reshape(ROWS, FB)
    out_ref[...] = (shared + dot(wcomb[0], back) + dot(wcomb[1], back)).astype(BF16)

    for copy in sends:
        copy.wait_send()


def local(
    tokens, expert_ids, combine_weight, old_plan, new_plan, gate_weight, up_weight, down_weight,
    shared_gate, shared_up, shared_down,
):
    dma = pltpu.SemaphoreType.DMA
    vmem = pltpu.VMEM
    return pl.pallas_call(
        kernel,
        out_shape=jax.ShapeDtypeStruct((TOK, FB), BF16),
        in_specs=[pl.BlockSpec(memory_space=pltpu.HBM)] * 11,
        out_specs=pl.BlockSpec(memory_space=pltpu.VMEM),
        scratch_shapes=[
            vmem((TOK, D), BF16),
            vmem((TOK, CH), BF16),
            vmem((8, TOK), jnp.int32),
            vmem((8, TOK), F32),
            pltpu.SMEM((SLOTS,), jnp.int32),
            pltpu.SMEM((SLOTS,), jnp.int32),
            vmem((D, 2 * HB), BF16),
            vmem((D, 2 * HB), BF16),
            vmem((2, HB, D), BF16),
            vmem((2, HB, D), BF16),
            vmem((2, NY, 16, FB), BF16),
            vmem((2, NY, 16, FB), BF16),
            vmem((2, NL, 16, FB), BF16),
            vmem((2, NX, 2, NL, 16, FB), BF16),
            vmem((2, ROWS, HB), BF16),
            vmem((2, TOK, HB), BF16),
            vmem((2, 6, TOK // 2, FB), BF16),
            vmem((2, 6, TOK // 2, FB), BF16),
            vmem((2, 2, TOK // 2, FB), F32),
            vmem((2, TOK, FB), F32),
            vmem((TOK, FB), BF16),
            vmem((TOK, FB), BF16),
            vmem((2, ROWS, FB), F32),
            vmem((2, 3, ROWS, FB), BF16),
            vmem((2, 3, ROWS, FB), BF16),
            vmem((2, NL, 16, FB), BF16),
            vmem((NZ, 16, FB), BF16),
            vmem((NY, 16, FB), BF16),
            vmem((NY, 16, FB), BF16),
            vmem((2, TOK, ROWS), BF16),
            dma((12,)),
            dma((2, 8)), dma((2, 8)),
            dma((2, 7)), dma((2, 7)),
            dma((12,)), dma((12,)),
            dma((2, 6)), dma((2, 6)),
            dma((2, 3)), dma((2, 3)),
            dma((2, 3)), dma((2, 3)),
            dma((16,)), dma((16,)),
            dma((1,)), dma((1,)),
            dma((8,)), dma((8,)),
        ],
        compiler_params=pltpu.CompilerParams(
            collective_id=0, has_side_effects=True, vmem_limit_bytes=60 * 2**20
        ),
        cost_estimate=pl.CostEstimate(flops=2 * 10**9, bytes_accessed=12 * 2**20, transcendentals=10**5),
    )(
        tokens, expert_ids.T, combine_weight.T, old_plan, new_plan, gate_weight, up_weight, down_weight,
        shared_gate, shared_up, shared_down,
    )


def solution(mesh):
    in_specs = (
        P("expert", None),
        P("expert", None),
        P("expert", None),
        P(),
        P(),
        P("expert", None, "dp"),
        P("expert", None, "dp"),
        P("expert", "dp", None),
        P(None, "dp"),
        P(None, "dp"),
        P("dp", None),
    )
    out_specs = P("expert", "dp")
    return jax.shard_map(local, mesh=mesh, in_specs=in_specs, out_specs=out_specs, check_vma=False)
```

```python
import jax
import jax.numpy as jnp
from jax import lax
from jax.experimental import pallas as pl
from jax.experimental.pallas import tpu as pltpu
from jax.sharding import PartitionSpec as P

MESH = pl.DeviceIdType.MESH
BF16 = jnp.bfloat16
F32 = jnp.float32

NX, NY, NZ, NL = 4, 8, 16, 8
TOK = 256
D = 4096
HB = 128
SLOTS = 64
ROWS = 128
CH = 512
FB = 256


def dot(a, b):
    return jnp.dot(a, b, preferred_element_type=F32)


def gated(g, u):
    return (g / (1.0 + jnp.exp(-g)) * u).astype(BF16)


def kernel(
    tokens_in, ids_in, cw_in, old_in, new_in, gate_in, up_in, down_in, sgate_in, sup_in, sdown_in,
    out_ref,
    tokens, chunk, ids, cw, old, new, wgu, swgu, down, sdown,
    gbuf, abuf, bbuf, xrows, hid, shid,
    s_send, s_recv, s_mid, s_own, z_send, z_recv,
    p_own, p_send, p_recv, rbuf, dbuf, ysend, ebuf, wcomb,
    lsem, y_ss, y_rs, z_ss, z_rs, a_ss, a_rs, b_ss, b_rs, x_ss, x_rs, r_ss, r_rs, v_ss, v_rs,
    t_ss, t_rs, u_ss, u_rs,
):
    d = lax.axis_index("dp")
    e = lax.axis_index("expert")
    x = lax.div(d, 4)
    zh = lax.rem(lax.div(d, 2), 2)
    c = lax.rem(d, 2)
    y = lax.div(e, NL)
    zl = lax.rem(e, NL)
    z = zh * NL + zl
    xa = x + 1 - 2 * lax.rem(x, 2)
    xb = 3 - x
    xo = lax.rem(x + 2, NX)
    oc = 1 - c

    def dev(x_, y_, z_, c_):
        return (x_ * 4 + lax.div(z_, NL) * 2 + c_, y_ * NL + lax.rem(z_, NL))

    sib = dev(x, y, z, oc)
    dev_a = dev(xa, y, z, c)
    dev_b = dev(xb, y, z, c)
    dev_o = dev(xo, y, z, c)
    across = (dev_a, dev_b, dev_o)
    places = (xa, xb, xo)

    def load(src, dst, i):
        copy = pltpu.make_async_copy(src, dst, lsem.at[i])
        copy.start()
        return copy

    l_old = load(old_in, old, 0)
    l_new = load(new_in, new, 1)
    l_ids = load(ids_in, ids, 2)
    l_cw = load(cw_in, cw, 3)
    l_chunk = load(tokens_in.at[:, pl.ds(pl.multiple_of(x * 1024 + c * CH, CH), CH)], chunk, 4)

    barrier = pltpu.get_barrier_semaphore()
    peers = [sib, dev_a, dev_b, dev_o]
    peers += [dev(x, lax.rem(y + r, NY), z, c) for r in range(1, NY)]
    peers += [dev(x, y, lax.rem(z + r, NZ), c) for r in range(1, NZ)]
    for peer in peers:
        pl.semaphore_signal(barrier, inc=1, device_id=peer, device_id_type=MESH)

    l_sg = load(sgate_in, swgu.at[:, pl.ds(0, HB)], 5)
    l_su = load(sup_in, swgu.at[:, pl.ds(HB, HB)], 6)
    l_tok = load(tokens_in, tokens, 7)

    sends = []

    def send(src, dst, ss, rs, peer):
        copy = pltpu.make_async_remote_copy(
            src_ref=src, dst_ref=dst, send_sem=ss, recv_sem=rs, device_id=peer, device_id_type=MESH
        )
        copy.start()
        sends.append(copy)

    def arrived(dst, ss, rs):
        pltpu.make_async_remote_copy(
            src_ref=dst, dst_ref=dst, send_sem=ss, recv_sem=rs, device_id=sib, device_id_type=MESH
        ).wait_recv()

    l_old.wait()
    l_new.wait()
    lane8 = lax.broadcasted_iota(jnp.int32, (8, ROWS), 1)
    slot8 = lax.div(lane8, 2)

    held = jnp.full((8, ROWS), -1, jnp.int32)
    for s in range(SLOTS):
        held = jnp.where(slot8 == s, old[s], held)
    kept = jnp.zeros((8, ROWS), jnp.bool_)
    for s in range(SLOTS):
        kept = kept | (held == new[s])
    held = jnp.where(kept, held, -1).astype(F32)[0:1, :]
    held = jnp.transpose(jnp.broadcast_to(held, (ROWS, ROWS))).astype(jnp.int32)
    held = jnp.concatenate([held, held], axis=1)
    l_ids.wait()
    l_cw.wait()
    match = jnp.zeros((ROWS, TOK), F32)
    weight = jnp.zeros((ROWS, TOK), F32)
    for k in range(8):
        hit = ids[k : k + 1, :] == held
        match = match + jnp.where(hit, 1.0, 0.0)
        weight = weight + jnp.where(hit, cw[k : k + 1, :], 0.0)
    upper = jnp.where(
        lax.broadcasted_iota(jnp.int32, (TOK, TOK), 0) < lax.broadcasted_iota(jnp.int32, (TOK, TOK), 1),
        1.0, 0.0,
    ).astype(BF16)
    before = dot(match.astype(BF16), upper)
    place = lax.rem(lax.broadcasted_iota(jnp.int32, (ROWS, TOK), 0), 2).astype(F32)
    here = jnp.where(before == place, 1.0, 0.0)
    pick = (match * here).astype(BF16)
    weight = weight * here
    row = lax.broadcasted_iota(jnp.int32, (ROWS, ROWS), 0)
    col = lax.broadcasted_iota(jnp.int32, (ROWS, ROWS), 1)
    swapped = lax.rem(lax.div(row, 2), 8) * 16 + lax.div(row, 16) * 2 + lax.rem(row, 2)
    swap = jnp.where(col == swapped, 1.0, 0.0).astype(BF16)

    l_chunk.wait()
    for f in range(2):
        gbuf[f] = dot(pick, chunk[:, f * FB : (f + 1) * FB]).astype(BF16).reshape(NY, 16, FB)
        abuf[f, y] = gbuf[f, y]
        if f == 0:
            pl.semaphore_wait(barrier, len(peers))
        for r in range(1, NY):
            to = lax.rem(y + r, NY)
            send(gbuf.at[f, to], abuf.at[f, y], y_ss.at[f, r], y_rs.at[f, r], dev(x, to, z, c))
    l_sd = load(sdown_in, sdown.at[c], 8)
    send(sdown_in, sdown.at[c], a_ss.at[0], a_rs.at[0], sib)
    l_g = load(gate_in.at[0], wgu.at[:, pl.ds(0, HB)], 9)
    l_u = load(up_in.at[0], wgu.at[:, pl.ds(HB, HB)], 10)

    weight = jnp.transpose(weight)
    high = weight.astype(BF16)
    wcomb[0] = high
    wcomb[1] = (weight - high.astype(F32)).astype(BF16)

    l_sg.wait()
    l_su.wait()
    l_tok.wait()
    both = dot(tokens[...], swgu[...])
    shid[c] = gated(both[:, :HB], both[:, HB:])
    send(shid.at[c], shid.at[c], a_ss.at[2], a_rs.at[2], sib)

    steps = [1, 15, 2, 14, 3, 13, 4 + 8 * c]
    for f in range(2):
        for r in range(1, NY):
            frm = lax.rem(y + NY - r, NY)
            arrived(abuf.at[f, frm], y_ss.at[f, r], y_rs.at[f, r])
        bbuf[f] = dot(swap, abuf[f].reshape(ROWS, FB)).astype(BF16).reshape(NL, 16, FB)
        for i, step in enumerate(steps):
            to = lax.rem(z + step, NZ)
            send(bbuf.at[f, lax.rem(to, NL)], xrows.at[c, x, f, zl], z_ss.at[f, i], z_rs.at[f, i], dev(x, y, to, c))
        xrows[c, x, f, zl] = bbuf[f, zl]
    l_d = load(down_in.at[0], down.at[c], 11)
    send(down_in.at[0], down.at[c], a_ss.at[1], a_rs.at[1], sib)

    l_sd.wait()
    arrived(sdown.at[oc], a_ss.at[0], a_rs.at[0])
    arrived(shid.at[oc], a_ss.at[2], a_rs.at[2])
    sh0 = shid[0]
    sh1 = shid[1]

    def columns(ref, core, x_, half):
        at = pl.multiple_of(x_ * 1024 + half * CH + c * FB, FB)
        return ref[core, :, pl.ds(at, FB)]

    def shared_part(x_, half):
        return dot(sh0, columns(sdown, 0, x_, half)) + dot(sh1, columns(sdown, 1, x_, half))

    HR = TOK // 2
    halves = (1 - zh, zh)

    def shared_first(k):
        part = shared_part(xo, halves[k]).astype(BF16)
        s_send[k, 0] = part[:HR]
        s_send[k, 1] = part[HR:]
        part = shared_part(xa, halves[k])
        s_send[k, 2] = part[:HR].astype(BF16)
        s_mid[k, 0] = part[HR:]
        part = shared_part(xb, halves[k])
        s_send[k, 3] = part[HR:].astype(BF16)
        s_mid[k, 1] = part[:HR]
        for i in range(4):
            send(s_send.at[k, i], s_recv.at[k, i], b_ss.at[k, i], b_rs.at[k, i], across[i % 2])
        s_own[k] = shared_part(x, halves[k])

    def shared_second(k):
        arrived(s_recv.at[k, 0], b_ss.at[k, 0], b_rs.at[k, 0])
        s_send[k, 5] = (s_mid[k, 1] + s_recv[k, 0].astype(F32)).astype(BF16)
        send(s_send.at[k, 5], s_recv.at[k, 5], b_ss.at[k, 5], b_rs.at[k, 5], dev_b)
        arrived(s_recv.at[k, 1], b_ss.at[k, 1], b_rs.at[k, 1])
        s_send[k, 4] = (s_mid[k, 0] + s_recv[k, 1].astype(F32)).astype(BF16)
        send(s_send.at[k, 4], s_recv.at[k, 4], b_ss.at[k, 4], b_rs.at[k, 4], dev_a)

    def shared_last(k):
        for i in range(2, 6):
            arrived(s_recv.at[k, i], b_ss.at[k, i], b_rs.at[k, i])
        s_own[k, :HR] = s_own[k, :HR] + s_recv[k, 2].astype(F32) + s_recv[k, 5].astype(F32)
        s_own[k, HR:] = s_own[k, HR:] + s_recv[k, 3].astype(F32) + s_recv[k, 4].astype(F32)

    shared_first(0)

    for f in range(2):
        for i, step in enumerate(steps):
            frm = lax.rem(z + NZ - step, NZ)
            arrived(xrows.at[c, x, f, lax.rem(frm, NL)], z_ss.at[f, i], z_rs.at[f, i])
        piece = xrows.at[c, x, f]
        for i in (2, 0, 1):
            send(piece, piece, x_ss.at[f, i], x_rs.at[f, i], across[i])
        send(piece, piece, a_ss.at[4 + f], a_rs.at[4 + f], sib)
        if f == 0:
            shared_second(0)

    l_g.wait()
    l_u.wait()

    def product(core, x_, f):
        at = pl.multiple_of(x_ * 1024 + core * CH + f * FB, FB)
        return dot(xrows[core, x_, f].reshape(ROWS, FB), wgu[pl.ds(at, FB), :])

    acc = product(c, x, 0) + product(c, x, 1)
    for f in range(2):
        for i in range(3):
            piece = xrows.at[c, places[i], f]
            arrived(piece, x_ss.at[f, i], x_rs.at[f, i])
            send(piece, piece, a_ss.at[6 + 3 * f + i], a_rs.at[6 + 3 * f + i], sib)
            acc = acc + product(c, places[i], f)
        if f == 0:
            shared_last(0)
            z_send[...] = s_own[0].astype(BF16)
            send(z_send, z_recv, t_ss.at[0], t_rs.at[0], dev(x, y, lax.rem(z + NL, NZ), c))
    shared_first(1)

    for f in range(2):
        arrived(xrows.at[oc, x, f], a_ss.at[4 + f], a_rs.at[4 + f])
        acc = acc + product(oc, x, f)
    for f in range(2):
        for i in range(3):
            arrived(xrows.at[oc, places[i], f], a_ss.at[6 + 3 * f + i], a_rs.at[6 + 3 * f + i])
            acc = acc + product(oc, places[i], f)
    hid[c] = gated(acc[:, :HB], acc[:, HB:])
    send(hid.at[c], hid.at[c], a_ss.at[3], a_rs.at[3], sib)

    l_d.wait()
    arrived(down.at[oc], a_ss.at[1], a_rs.at[1])
    arrived(hid.at[oc], a_ss.at[3], a_rs.at[3])
    h0 = hid[0]
    h1 = hid[1]

    def route_part(x_, half):
        return dot(h0, columns(down, 0, x_, half)) + dot(h1, columns(down, 1, x_, half))

    for k in range(2):
        half = halves[k]
        for i in (2, 0, 1):
            p_send[k, i] = route_part(places[i], half).astype(BF16)
            send(p_send.at[k, i], p_recv.at[k, i], r_ss.at[k, i], r_rs.at[k, i], across[i])
        p_own[k] = route_part(x, half)

    shared_second(1)
    for k in range(2):
        half = halves[k]
        total = p_own[k]
        for i in range(3):
            arrived(p_recv.at[k, i], r_ss.at[k, i], r_rs.at[k, i])
            total = total + p_recv[k, i].astype(F32)
        rbuf[k] = total.astype(BF16).reshape(NL, 16, FB)
        for r in range(k, NL):
            to = lax.rem(zl + r, NL)
            at = (1 - k) * NL + r
            send(rbuf.at[k, to], dbuf.at[z], v_ss.at[at], v_rs.at[at], dev(x, y, half * NL + to, c))
    dbuf[z] = rbuf[1, zl]

    shared_last(1)
    arrived(z_recv, t_ss.at[0], t_rs.at[0])
    shared = s_own[1] + z_recv[...].astype(F32)

    for k in range(2):
        half = halves[k]
        for r in range(k, NL):
            frm = half * NL + lax.rem(zl + NL - r, NL)
            at = (1 - k) * NL + r
            arrived(dbuf.at[frm], v_ss.at[at], v_rs.at[at])
    total = (dbuf[0:NL].astype(F32) + dbuf[NL:NZ].astype(F32)).astype(BF16)
    ysend[...] = dot(swap, total.reshape(ROWS, FB)).astype(BF16).reshape(NY, 16, FB)
    for r in range(1, NY):
        to = lax.rem(y + r, NY)
        send(ysend.at[to], ebuf.at[y], u_ss.at[r], u_rs.at[r], dev(x, to, z, c))
    ebuf[y] = ysend[y]
    for r in range(1, NY):
        frm = lax.rem(y + NY - r, NY)
        arrived(ebuf.at[frm], u_ss.at[r], u_rs.at[r])
    back = ebuf[...].reshape(ROWS, FB)
    out_ref[...] = (shared + dot(wcomb[0], back) + dot(wcomb[1], back)).astype(BF16)

    for copy in sends:
        copy.wait_send()


def local(
    tokens, expert_ids, combine_weight, old_plan, new_plan, gate_weight, up_weight, down_weight,
    shared_gate, shared_up, shared_down,
):
    dma = pltpu.SemaphoreType.DMA
    vmem = pltpu.VMEM
    return pl.pallas_call(
        kernel,
        out_shape=jax.ShapeDtypeStruct((TOK, FB), BF16),
        in_specs=[pl.BlockSpec(memory_space=pltpu.HBM)] * 11,
        out_specs=pl.BlockSpec(memory_space=pltpu.VMEM),
        scratch_shapes=[
            vmem((TOK, D), BF16),
            vmem((TOK, CH), BF16),
            vmem((8, TOK), jnp.int32),
            vmem((8, TOK), F32),
            pltpu.SMEM((SLOTS,), jnp.int32),
            pltpu.SMEM((SLOTS,), jnp.int32),
            vmem((D, 2 * HB), BF16),
            vmem((D, 2 * HB), BF16),
            vmem((2, HB, D), BF16),
            vmem((2, HB, D), BF16),
            vmem((2, NY, 16, FB), BF16),
            vmem((2, NY, 16, FB), BF16),
            vmem((2, NL, 16, FB), BF16),
            vmem((2, NX, 2, NL, 16, FB), BF16),
            vmem((2, ROWS, HB), BF16),
            vmem((2, TOK, HB), BF16),
            vmem((2, 6, TOK // 2, FB), BF16),
            vmem((2, 6, TOK // 2, FB), BF16),
            vmem((2, 2, TOK // 2, FB), F32),
            vmem((2, TOK, FB), F32),
            vmem((TOK, FB), BF16),
            vmem((TOK, FB), BF16),
            vmem((2, ROWS, FB), F32),
            vmem((2, 3, ROWS, FB), BF16),
            vmem((2, 3, ROWS, FB), BF16),
            vmem((2, NL, 16, FB), BF16),
            vmem((NZ, 16, FB), BF16),
            vmem((NY, 16, FB), BF16),
            vmem((NY, 16, FB), BF16),
            vmem((2, TOK, ROWS), BF16),
            dma((12,)),
            dma((2, 8)), dma((2, 8)),
            dma((2, 7)), dma((2, 7)),
            dma((12,)), dma((12,)),
            dma((2, 6)), dma((2, 6)),
            dma((2, 3)), dma((2, 3)),
            dma((2, 3)), dma((2, 3)),
            dma((16,)), dma((16,)),
            dma((1,)), dma((1,)),
            dma((8,)), dma((8,)),
        ],
        compiler_params=pltpu.CompilerParams(
            collective_id=0, has_side_effects=True, vmem_limit_bytes=60 * 2**20
        ),
        cost_estimate=pl.CostEstimate(flops=2 * 10**9, bytes_accessed=12 * 2**20, transcendentals=10**5),
    )(
        tokens, expert_ids.T, combine_weight.T, old_plan, new_plan, gate_weight, up_weight, down_weight,
        shared_gate, shared_up, shared_down,
    )


def solution(mesh):
    in_specs = (
        P("expert", None),
        P("expert", None),
        P("expert", None),
        P(),
        P(),
        P("expert", None, "dp"),
        P("expert", None, "dp"),
        P("expert", "dp", None),
        P(None, "dp"),
        P(None, "dp"),
        P("dp", None),
    )
    out_specs = P("expert", "dp")
    return jax.shard_map(local, mesh=mesh, in_specs=in_specs, out_specs=out_specs, check_vma=False)
```
